256 devices in a mesh: dom: 64 (over y, z, core), fsdp: 4 (over x).
Axes of the slice: x: 4, y: 4, z: 8, core: 2. Of those that a mesh axis runs over, the one named last changes fastest.
Arguments:
- hidden: bfloat16 [65536, 1024], P(('dom', 'fsdp')), may hold values from -24 to 24
- history: bfloat16 [65536, 1024], P(('dom', 'fsdp')), may hold values from -6 to 6
- cotangent: bfloat16 [65536, 1024], P(('dom', 'fsdp')), may hold values from -6 to 6
- weight: bfloat16 [4096, 1024], P('fsdp'), may hold values from -0.09375 to 0.09375
- send_index: int32 [256, 256, 4], P(('dom', 'fsdp')), may hold values from 0 to 255
- send_count: int32 [256, 256], P(('dom', 'fsdp')), may hold values from 0 to 4, as said below
- tile_values: bfloat16 [256, 24, 128, 128], P(('dom', 'fsdp')), may hold values from -0.3125 to 0.3125
- tile_row: int32 [256, 24], P(('dom', 'fsdp')), may hold values from 0 to 1
- tile_col: int32 [256, 24], P(('dom', 'fsdp')), may hold values from 0 to 15
- tile_rel: int32 [256, 24], P(('dom', 'fsdp')), may hold values from 0 to 3
- tile_count: int32 [256], P(('dom', 'fsdp')), may hold values from 12 to 24, as said below
Outputs:
- output: bfloat16 [65536, 1024], P(('dom', 'fsdp'))
- grad_hidden: float32 [65536, 1024], P(('dom', 'fsdp'))
- grad_weight: float32 [4096, 1024], P(('dom', 'fsdp'))
The draws below stay inside these ranges and needn't reach their ends.
Inputs may be any that keep to these rules, and one draw needn't show every extreme that they name: send_count is 0 wherever sender and receiver lie in the same partition; for some receivers every sender of another partition sends all 4 rows. `tile_count`: tiles at or past a device's count are ignored; some device uses all 24.
All inputs are finite; a program needn't handle non-finite values.
Results may differ from the reference program's by a relative error of at most 0.0075.
Values may be sent and summed in bfloat16 or wider, within the bound.
No kernel may reach another device: no remote copies, remote signals or barrier semaphores. Data moves between devices by JAX's collectives and lax.ppermute only.
A program may use at most 128 MiB of HBM per device.

```python
import jax
import jax.numpy as jnp
from jax import lax

D = 1024
RELS = 4
BLOCK = 128
ROWS_DEV = 256
SLOTS = 4
TILE_ROW = 12
SHARDS = 256
NODES = 65536
ROW_BLOCKS = 2
TILES = 24
COL_BLOCKS = 16
N_FSDP = 4


def draw_send_count(key, part):
    key_crowd, key_base, key_pick = jax.random.split(jax.random.fold_in(key, 11), 3)
    crowded = jax.random.randint(key_crowd, (SHARDS,), 0, 4) == 0
    forced = jax.random.randint(key_pick, (), 0, SHARDS)
    crowded = crowded | (jnp.arange(SHARDS) == forced)
    baseline = jax.random.randint(key_base, (SHARDS, SHARDS), 0, SLOTS + 1)
    counts = jnp.where(crowded[None, :], SLOTS, baseline)
    dom_ids = jnp.arange(SHARDS) // N_FSDP
    counts = jnp.where(dom_ids[:, None] == dom_ids[None, :], 0, counts)
    return counts.astype(jnp.int32)


def draw_tile_count(key, part):
    key_base, key_pick = jax.random.split(jax.random.fold_in(key, 23), 2)
    totals = jax.random.randint(key_base, (SHARDS,), TILES // 2, TILES + 1)
    forced = jax.random.randint(key_pick, (), 0, SHARDS)
    totals = jnp.where(jnp.arange(SHARDS) == forced, TILES, totals)
    return totals.astype(jnp.int32)


def touch_ends(drawn, key, low, largest):
    index_at = [jax.random.randint(jax.random.fold_in(key, axis), (), 0, length) for axis, length in enumerate(drawn.shape)]
    main_axis = drawn.shape.index(max(drawn.shape))
    neighbour = index_at[:main_axis] + [(index_at[main_axis] + 1) % drawn.shape[main_axis]] + index_at[main_axis + 1:]
    return drawn.at[tuple(index_at)].set(low).at[tuple(neighbour)].set(largest)


def with_spikes(drawn, stream_key, source, target, parts, factor):
    owner, partner = [(jnp.arange(drawn.shape[position]) // (drawn.shape[position] // parts)).reshape([-1 if axis == position else 1 for axis in range(drawn.ndim)]) for position in (source, target)]
    chosen = jax.random.permutation(stream_key, parts)[partner]
    strong = (owner == chosen) | (owner == (partner + parts // 2) % parts)
    return jnp.where(strong, factor * drawn, drawn)


def levels(key, extent, pieces, least, top_value):
    gain = 1.0
    for axis_at, blocks in pieces:
        heights = jax.random.uniform(jax.random.fold_in(jax.random.fold_in(key, 6), axis_at), (blocks,), jnp.float32, least / len(pieces), top_value / len(pieces))
        gain = gain * jnp.repeat(jnp.exp(heights), extent[axis_at] // blocks).reshape((-1,) + (1,) * (len(extent) - 1 - axis_at))
    return gain


def noise(stream_key, shape, spread, reach, cuts=(), held_as=jnp.bfloat16):
    level = levels(stream_key, shape, cuts, -0.22, 0.18) if cuts else 1.0
    drawn = jax.random.normal(stream_key, shape, jnp.float32) * spread * level
    return jnp.minimum(jnp.maximum(drawn, -reach), reach).astype(held_as)


def heavy_noise(own_key, shape, width, most, pieces, heavy, held_as=jnp.bfloat16):
    array = width * jax.random.normal(own_key, shape, jnp.float32)
    if pieces:
        array = array * levels(own_key, shape, pieces, -0.22, 0.18)
    return jnp.clip(with_spikes(array, jax.random.fold_in(own_key, 3), *heavy), -most, most).astype(held_as)


def setup_inputs(seed: int = 0) -> dict:
    splits = jax.random.split(jax.random.key(seed), 12)
    hidden = heavy_noise(splits[0], (NODES, D), 1.0, 24.0, ((0, 256),), (0, 1, 256, 6.0))
    history = noise(splits[1], (NODES, D), 1.0, 6.0, ((0, 256),))
    cotangent = noise(splits[2], (NODES, D), 1.0, 6.0, ((0, 256),))
    weight = noise(splits[3], (RELS * D, D), (RELS * D) ** -0.5, 0.09375, ((0, 4),))
    send_index = touch_ends(jax.random.randint(splits[4], (SHARDS, SHARDS, SLOTS), 0, ROWS_DEV), jax.random.fold_in(splits[4], 1), 0, ROWS_DEV - 1).astype(jnp.int32)
    send_count = draw_send_count(jax.random.fold_in(splits[11], 71), 0)
    tile_values = noise(splits[6], (SHARDS, TILES, BLOCK, BLOCK), (BLOCK * TILE_ROW // RELS) ** -0.5, 0.3125, ((0, 256),))
    tile_row = touch_ends(jax.random.randint(splits[7], (SHARDS, TILES), 0, ROW_BLOCKS), jax.random.fold_in(splits[7], 1), 0, ROW_BLOCKS - 1).astype(jnp.int32)
    tile_col = touch_ends(jax.random.randint(splits[8], (SHARDS, TILES), 0, COL_BLOCKS), jax.random.fold_in(splits[8], 1), 0, COL_BLOCKS - 1).astype(jnp.int32)
    tile_rel = touch_ends(jax.random.randint(splits[9], (SHARDS, TILES), 0, RELS), jax.random.fold_in(splits[9], 1), 0, RELS - 1).astype(jnp.int32)
    tile_count = draw_tile_count(jax.random.fold_in(splits[11], 71), 0)
    return dict(hidden=hidden, history=history, cotangent=cotangent, weight=weight, send_index=send_index, send_count=send_count, tile_values=tile_values, tile_row=tile_row, tile_col=tile_col, tile_rel=tile_rel, tile_count=tile_count)


def gelu_tanh(values):
    return jax.nn.gelu(values, approximate=True)

def reference(hidden, history, cotangent, weight, send_index, send_count, tile_values, tile_row, tile_col, tile_rel, tile_count):
    part_size = N_FSDP * ROWS_DEV
    row_blocks = ROWS_DEV // BLOCK
    local_blocks = part_size // BLOCK
    tile_slots = tile_row.shape[1]
    sources = jnp.arange(SHARDS, dtype=jnp.int32)
    slot_ids = jnp.arange(SLOTS, dtype=jnp.int32)
    tile_ids = jnp.arange(tile_slots, dtype=jnp.int32)
    target_ids = jnp.arange(row_blocks * RELS, dtype=jnp.int32)
    block_ids = jnp.arange(local_blocks, dtype=jnp.int32)
    highest = lax.Precision.HIGHEST

    def device_step(running, device):
        grad_panel, grad_nodes = running
        dom_start = device // N_FSDP * part_size
        partition = lax.dynamic_slice_in_dim(hidden, dom_start, part_size, 0)
        wanted = lax.dynamic_index_in_dim(send_index, device, 1, keepdims=False)
        counts = lax.dynamic_index_in_dim(send_count, device, 1, keepdims=False)
        global_rows = (sources[:, None] * ROWS_DEV + wanted).reshape(-1).astype(jnp.int32)
        fetched = jnp.take(history, global_rows, axis=0).reshape(SHARDS, SLOTS, D)
        usable = slot_ids[None, :] < counts[:, None]
        fetched = jnp.where(usable[:, :, None], fetched, jnp.zeros_like(fetched))
        columns = jnp.concatenate([partition, fetched.reshape(SHARDS * SLOTS, D)], 0).reshape(-1, BLOCK, D)
        values = tile_values[device].astype(jnp.float32)
        row_ids = tile_row[device]
        col_ids = tile_col[device]
        rel_ids = tile_rel[device]
        active = tile_ids < tile_count[device]
        target = row_ids * RELS + rel_ids
        picked = columns[col_ids].astype(jnp.float32)
        products = jnp.einsum('tij,tjd->tid', values, picked, precision=highest)
        onehot = jnp.where((target[:, None] == target_ids[None, :]) & active[:, None], 1.0, 0.0).astype(jnp.float32)
        totals = jnp.einsum('ts,tid->sid', onehot, products, precision=highest)
        stacked = totals.reshape(row_blocks, RELS, BLOCK, D).transpose(0, 2, 1, 3).reshape(ROWS_DEV, RELS * D).astype(jnp.bfloat16)
        own_rows = lax.dynamic_slice_in_dim(hidden, device * ROWS_DEV, ROWS_DEV, 0)
        preact = jnp.dot(stacked, weight, preferred_element_type=jnp.float32)
        activated, pullback = jax.vjp(gelu_tanh, preact)
        output = (own_rows.astype(jnp.float32) + activated).astype(jnp.bfloat16)
        upstream = lax.dynamic_slice_in_dim(cotangent, device * ROWS_DEV, ROWS_DEV, 0).astype(jnp.float32)
        grad_preact = pullback(upstream)[0].astype(jnp.bfloat16)
        grad_stacked = lax.dot_general(grad_preact, weight, (((1,), (1,)), ((), ())), preferred_element_type=jnp.float32).astype(jnp.bfloat16)
        grad_panel = grad_panel + lax.dot_general(stacked, grad_preact, (((0,), (0,)), ((), ())), preferred_element_type=jnp.float32)
        grad_blocks = grad_stacked.reshape(row_blocks, BLOCK, RELS, D).transpose(0, 2, 1, 3).reshape(row_blocks * RELS, BLOCK, D)
        pulled = jnp.einsum('tij,tid->tjd', values, grad_blocks[target].astype(jnp.float32), precision=highest)
        landing = jnp.where((col_ids[:, None] == block_ids[None, :]) & active[:, None], 1.0, 0.0).astype(jnp.float32)
        node_term = jnp.einsum('tc,tjd->cjd', landing, pulled, precision=highest).reshape(part_size, D)
        previous = lax.dynamic_slice_in_dim(grad_nodes, dom_start, part_size, 0)
        grad_nodes = lax.dynamic_update_slice_in_dim(grad_nodes, previous + node_term, dom_start, 0)
        return ((grad_panel, grad_nodes), output)
    start_state = (jnp.zeros((RELS * D, D), jnp.float32), jnp.zeros((NODES, D), jnp.float32))
    final_state, outputs = lax.scan(device_step, start_state, jnp.arange(SHARDS, dtype=jnp.int32))
    grad_panel, grad_nodes = final_state
    grad_hidden = cotangent.astype(jnp.float32) + grad_nodes
    return (outputs.reshape(NODES, D), grad_hidden, grad_panel)
```

```python
import functools

import jax
import jax.numpy as jnp
from jax import lax
from jax.experimental import pallas as pl
from jax.experimental.pallas import tpu as pltpu
from jax.sharding import Mesh, PartitionSpec as P

ROWS = 256
WIDTH = 1024
HALF = 512
RELS = 4
BLOCK = 128
TILES = 24
LOCAL = 8
ALL = ("y", "z", "c", "x")
F32 = jnp.float32
BF16 = jnp.bfloat16
NEXT = [(i, (i + 1) % 4) for i in range(4)]
BACK = [(i, (i + 3) % 4) for i in range(4)]
VMEM = pl.BlockSpec(memory_space=pltpu.VMEM)
HBM = pl.BlockSpec(memory_space=pl.ANY)
SMEM = pl.BlockSpec(memory_space=pltpu.SMEM)
GELU_A = 0.7978845608028654
GELU_B = 0.044715


def panel_copies(core, pieces, panel, sems):
    own, right, right_far, left, left_far, op_a, op_a_far, op_b, op_b_far = pieces
    near = pl.multiple_of(core * HALF, HALF)
    far = pl.multiple_of((1 - core) * HALF, HALF)
    quarter = HALF // 2
    plan = (
        ((own, 0, 0, WIDTH),),
        ((right, 1, near, HALF), (right_far, 1, far, HALF)),
        (
            (op_a, 2, near, quarter),
            (op_b, 2, near + quarter, quarter),
            (op_a_far, 2, far, quarter),
            (op_b_far, 2, far + quarter, quarter),
        ),
        ((left, 3, near, HALF), (left_far, 3, far, HALF)),
    )
    copies, at = [], 0
    for group in plan:
        made = []
        for source, slot, start, size in group:
            made.append(
                pltpu.make_async_copy(source, panel.at[slot, pl.ds(start, size)], sems.at[at])
            )
            at += 1
        copies.append(made)
    return copies


def forward_kernel(
    row_ref, col_ref, rel_ref, count_ref, place_ref,
    p0, p1, p2, p3, arrived,
    w0, w1, w2, w3, w4, w5, w6, w7, w8,
    tiles_ref, hidden_ref, cot_ref,
    out_ref, grad_ref, mine_ref, send_ref,
    cols, totals, stacked, panel, col_sems, panel_sems,
):
    core, x = place_ref[0], place_ref[1]
    col_copies = [
        pltpu.make_async_copy(part, cols.at[pl.ds(2 * j, 2)], col_sems.at[j])
        for j, part in enumerate((p0, p1, p2, p3))
    ]
    col_copies.append(pltpu.make_async_copy(arrived, cols.at[pl.ds(LOCAL, 8)], col_sems.at[4]))
    weights = panel_copies(core, (w0, w1, w2, w3, w4, w5, w6, w7, w8), panel, panel_sems)
    for copy in col_copies:
        copy.start()
    for group in weights:
        for copy in group:
            copy.start()
    totals[...] = jnp.zeros_like(totals)
    for copy in col_copies:
        copy.wait()
    count = count_ref[0]

    def one_tile(i):
        col = col_ref[i]
        slot = jnp.where(
            col < LOCAL, 2 * ((col // 2 + 4 - x) % 4) + col % 2, col
        )
        target = jnp.where(i < count, row_ref[i] * RELS + rel_ref[i], 2 * RELS)
        totals[target] += jnp.dot(tiles_ref[i], cols[slot], preferred_element_type=F32)

    def four_tiles(step, carry):
        for k in range(4):
            one_tile(step * 4 + k)
        return carry

    lax.fori_loop(0, TILES // 4, four_tiles, 0)
    for rel in range(RELS):
        for block in range(2):
            stacked[rel, block * BLOCK : (block + 1) * BLOCK, :] = totals[
                block * RELS + rel
            ].astype(BF16)
    near = pl.multiple_of(core * HALF, HALF)
    far = pl.multiple_of((1 - core) * HALF, HALF)
    for rel in range(RELS):
        mine_ref[rel] = stacked[rel, :, pl.ds(near, HALF)]
        send_ref[rel] = stacked[rel, :, pl.ds(far, HALF)]
    for group in weights:
        for copy in group:
            copy.wait()
    for n in range(4):
        cut = slice(n * 256, (n + 1) * 256)
        v = jnp.zeros((ROWS, 256), F32)
        for j in range(4):
            v += jnp.dot(stacked[(x + j) % 4], panel[j, :, cut], preferred_element_type=F32)
        square = v * v
        t = jnp.tanh(GELU_A * (v + GELU_B * (square * v)))
        cdf = 0.5 * (1.0 + t)
        slope = cdf + (0.5 * v) * (1.0 - t * t) * (GELU_A * (1.0 + (3.0 * GELU_B) * square))
        out_ref[:, cut] = (hidden_ref[:, cut].astype(F32) + v * cdf).astype(BF16)
        grad_ref[:, cut] = (cot_ref[:, cut].astype(F32) * slope).astype(BF16)


def backward_kernel(
    row_ref, col_ref, rel_ref, count_ref, place_ref,
    w0, w1, w2, w3, w4, w5, w6, w7, w8,
    tiles_ref, grad_ref,
    own_ref, right_a, right_b, left_a, left_b, opp_a, opp_b,
    grads, nodes, panel, panel_sems,
):
    core, x = place_ref[0], place_ref[1]
    weights = panel_copies(core, (w0, w1, w2, w3, w4, w5, w6, w7, w8), panel, panel_sems)
    for group in weights:
        for copy in group:
            copy.start()
    nodes[...] = jnp.zeros_like(nodes)
    for j in range(4):
        for copy in weights[j]:
            copy.wait()
        rel = (x + j) % 4
        for n in range(4):
            cut = slice(n * 256, (n + 1) * 256)
            part = lax.dot_general(
                grad_ref[...], panel[j, cut, :], (((1,), (1,)), ((), ())),
                preferred_element_type=F32,
            ).astype(BF16)
            grads[rel, :, cut] = part[:BLOCK]
            grads[RELS + rel, :, cut] = part[BLOCK:]
    count = count_ref[0]

    def one_tile(i):
        col = col_ref[i]
        target = jnp.where((i < count) & (col < LOCAL), col, LOCAL)
        nodes[target] += lax.dot_general(
            tiles_ref[i], grads[row_ref[i] * RELS + rel_ref[i]], (((0,), (0,)), ((), ())),
            preferred_element_type=F32,
        )

    def four_tiles(step, carry):
        for k in range(4):
            one_tile(step * 4 + k)
        return carry

    lax.fori_loop(0, TILES // 4, four_tiles, 0)
    own_ref[:BLOCK] = nodes[2 * x]
    own_ref[BLOCK:] = nodes[2 * x + 1]
    for j, (half_a, half_b) in ((1, (right_a, right_b)), (2, (opp_a, opp_b)), (3, (left_a, left_b))):
        owner = (x + j) % 4
        half_a[...] = nodes[2 * owner].astype(BF16)
        half_b[...] = nodes[2 * owner + 1].astype(BF16)


def panel_grad_kernel(parts, place_ref, mine_ref, came_ref, grad_ref, grad_came_ref, *outs):
    y = place_ref[2]
    for (j, first, size), out in zip(parts, outs):
        rel = (y + j) % 4
        for start in range(0, size, 256):
            cut = slice(first + start, first + start + 256)
            part = lax.dot_general(
                mine_ref[rel, :, cut], grad_ref[...], (((0,), (0,)), ((), ())),
                preferred_element_type=F32,
            ) + lax.dot_general(
                came_ref[rel, :, cut], grad_came_ref[...], (((0,), (0,)), ((), ())),
                preferred_element_type=F32,
            )
            out[start : start + 256] = part.astype(out.dtype)


def struct(shape, dtype=BF16):
    return jax.ShapeDtypeStruct(shape, dtype)


def cost(flops, moved):
    return pl.CostEstimate(flops=flops, bytes_accessed=moved, transcendentals=0)


def params(mib=60):
    return pltpu.CompilerParams(vmem_limit_bytes=mib * 2**20)


def panel_grad(parts, dtypes, operands):
    return pl.pallas_call(
        functools.partial(panel_grad_kernel, parts),
        out_shape=[struct((size, WIDTH), d) for (_, _, size), d in zip(parts, dtypes)],
        in_specs=[SMEM] + [VMEM] * 4,
        out_specs=[VMEM] * len(parts),
        compiler_params=params(),
        cost_estimate=cost(2 * 512 * WIDTH * sum(p[2] for p in parts), 6 << 20),
    )(*operands)


def add(a, b):
    return (a.astype(F32) + b.astype(F32)).astype(BF16)


def ring_sum(axis, own, right, left, opposite):
    (right_a, right_b), (left_a, left_b), (opp_a, opp_b) = right, left, opposite
    via_left = lax.ppermute(opp_a, axis, NEXT)
    via_right = lax.ppermute(opp_b, axis, BACK)
    got_lb = lax.ppermute(right_b, axis, NEXT)
    got_ra = lax.ppermute(left_a, axis, BACK)
    got_la = lax.ppermute(add(right_a, via_left), axis, NEXT)
    got_rb = lax.ppermute(add(left_b, via_right), axis, BACK)
    half = own.shape[0] // 2
    top = own[:half] + got_la.astype(F32) + got_ra.astype(F32)
    low = own[half:] + got_lb.astype(F32) + got_rb.astype(F32)
    return top, low


def on_device(
    hidden, history, cotangent, weight, send_index, send_count,
    tile_values, tile_row, tile_col, tile_rel, tile_count,
):
    core, x, y, z = (lax.axis_index(a) for a in ("c", "x", "y", "z"))
    place = jnp.stack([core, x, y, z]).astype(jnp.int32)
    slots = send_index.shape[2]
    peers = send_index.shape[1]

    usable = jnp.arange(slots, dtype=jnp.int32)[None, :] < send_count[0][:, None]
    wanted = jnp.where(usable, send_index[0], -1).reshape(-1)
    picks = (wanted[:, None] == jnp.arange(ROWS, dtype=jnp.int32)[None, :]).astype(BF16)
    fetched = jnp.dot(picks, history, preferred_element_type=F32).astype(BF16)
    arrived = lax.all_to_all(
        fetched.reshape(peers, slots, WIDTH), ALL, split_axis=0, concat_axis=0, tiled=True
    ).reshape(LOCAL, BLOCK, WIDTH)

    p0 = hidden.reshape(2, BLOCK, WIDTH)
    p3 = lax.ppermute(p0, "x", NEXT)
    p1 = lax.ppermute(p0, "x", BACK)
    p2 = jnp.concatenate(
        [lax.ppermute(p3[:1], "x", NEXT), lax.ppermute(p1[1:], "x", BACK)], 0
    )

    half = lax.dynamic_slice_in_dim(weight, core * HALF, HALF, 0)
    left = lax.ppermute(half, "x", NEXT)
    right = lax.ppermute(half, "x", BACK)
    op_a = lax.ppermute(left[: HALF // 2], "x", NEXT)
    op_b = lax.ppermute(right[HALF // 2 :], "x", BACK)
    swap = lambda a: lax.ppermute(a, "c", [(0, 1), (1, 0)])
    panel = (weight, right, swap(right), left, swap(left), op_a, swap(op_a), op_b, swap(op_b))

    ids = (tile_row[0], tile_col[0], tile_rel[0], tile_count, place)
    values = tile_values[0]
    output, grad_preact, mine, to_send = pl.pallas_call(
        forward_kernel,
        out_shape=[
            struct((ROWS, WIDTH)),
            struct((ROWS, WIDTH)),
            struct((RELS, ROWS, HALF)),
            struct((RELS, ROWS, HALF)),
        ],
        in_specs=[SMEM] * 5 + [HBM] * 14 + [VMEM] * 3,
        out_specs=[VMEM] * 4,
        scratch_shapes=[
            pltpu.VMEM((16, BLOCK, WIDTH), BF16),
            pltpu.VMEM((2 * RELS + 1, BLOCK, WIDTH), F32),
            pltpu.VMEM((RELS, ROWS, WIDTH), BF16),
            pltpu.VMEM((RELS, WIDTH, WIDTH), BF16),
            pltpu.SemaphoreType.DMA((5,)),
            pltpu.SemaphoreType.DMA((9,)),
        ],
        compiler_params=params(),
        cost_estimate=cost(3 * 10**9, 20 << 20),
    )(*ids, p0, p1, p2, p3, arrived, *panel, values, hidden, cotangent)

    came = swap(to_send)
    grad_came = swap(grad_preact)

    own, ra, rb, la, lb, oa, ob = pl.pallas_call(
        backward_kernel,
        out_shape=[struct((ROWS, WIDTH), F32)] + [struct((BLOCK, WIDTH))] * 6,
        in_specs=[SMEM] * 5 + [HBM] * 9 + [VMEM] * 2,
        out_specs=[VMEM] * 7,
        scratch_shapes=[
            pltpu.VMEM((2 * RELS, BLOCK, WIDTH), BF16),
            pltpu.VMEM((LOCAL + 1, BLOCK, WIDTH), F32),
            pltpu.VMEM((RELS, WIDTH, WIDTH), BF16),
            pltpu.SemaphoreType.DMA((9,)),
        ],
        compiler_params=params(),
        cost_estimate=cost(3 * 10**9, 16 << 20),
    )(*ids, *panel, values, grad_preact)

    operands = (place, mine, came, grad_preact, grad_came)
    g_oa, g_ob = panel_grad(((2, 0, 256), (2, 256, 256)), (BF16,) * 2, operands)
    g_rb, g_la, g_ra, g_lb, g_own = panel_grad(
        ((1, 256, 256), (3, 0, 256), (1, 0, 256), (3, 256, 256), (0, 0, 512)),
        (BF16,) * 4 + (F32,),
        operands,
    )
    top, low = ring_sum("y", g_own, (g_ra, g_rb), (g_la, g_lb), (g_oa, g_ob))
    node_top, node_low = ring_sum("x", own, (ra, rb), (la, lb), (oa, ob))
    grad_hidden = cotangent.astype(F32) + jnp.concatenate([node_top, node_low], 0)

    top, low = (a.reshape(4, 4, 16, WIDTH) for a in (top, low))
    chunk = lambda a, j: lax.dynamic_index_in_dim(a, (x + j) % 4, 1, keepdims=False)
    own_x = jnp.concatenate([chunk(top, 0), chunk(low, 0)], 0)
    pair = lambda j: tuple(chunk(a, j).astype(BF16) for a in (top, low))
    sum_top, sum_low = ring_sum("x", own_x, pair(1), pair(3), pair(2))
    pieces = jnp.concatenate([sum_top, sum_low], 0)

    grad_weight = jnp.zeros((16, WIDTH), F32)
    for j in range(8):
        route = []
        for at in range(8):
            for c in range(2):
                k = at ^ j
                route.append((at * 2 + c, (c * 4 + k // 2) * 2 + k % 2))
        piece = lax.dynamic_index_in_dim(pieces, z ^ j, 0, keepdims=False).astype(BF16)
        grad_weight += lax.ppermute(piece, ("z", "c"), route).astype(F32)
    return (output, grad_hidden, grad_weight)


def solution(mesh):
    physical = Mesh(mesh.devices.reshape(4, 8, 2, 4), ALL)
    rows = P(ALL, None)
    return jax.shard_map(
        on_device,
        mesh=physical,
        in_specs=(
            rows, rows, rows, P("x", None), P(ALL, None, None), rows,
            P(ALL, None, None, None), rows, rows, rows, P(ALL),
        ),
        out_specs=(rows, rows, rows),
        check_vma=False,
    )
```

```python
import functools

import jax
import jax.numpy as jnp
from jax import lax
from jax.experimental import pallas as pl
from jax.experimental.pallas import tpu as pltpu
from jax.sharding import Mesh, PartitionSpec as P

ROWS = 256
WIDTH = 1024
HALF = 512
RELS = 4
BLOCK = 128
TILES = 24
LOCAL = 8
ALL = ("y", "z", "c", "x")
F32 = jnp.float32
BF16 = jnp.bfloat16
NEXT = [(i, (i + 1) % 4) for i in range(4)]
BACK = [(i, (i + 3) % 4) for i in range(4)]
VMEM = pl.BlockSpec(memory_space=pltpu.VMEM)
HBM = pl.BlockSpec(memory_space=pl.ANY)
SMEM = pl.BlockSpec(memory_space=pltpu.SMEM)
GELU_A = 0.7978845608028654
GELU_B = 0.044715
Z_STEPS = 2


def panel_copies(core, y, pieces, panel, sems):
    near = core * HALF
    far = (1 - core) * HALF
    strip = HALF // 4
    plan = [(pieces[0], 0, 1, 0, WIDTH)]
    for base, side in ((near, pieces[1:6]), (far, pieces[6:11])):
        for piece, step, start, size in (
            (side[0], 0, 0, strip),
            (side[1], 3, 0, strip),
            (side[2], 1, 0, strip),
            (side[3], 2, 0, strip // 2),
            (side[4], 2, strip // 2, strip // 2),
        ):
            first = base + ((y + step) % 4) * strip + start
            plan.append((piece, 1, 3, pl.multiple_of(first, strip // 2), size))
    return [
        pltpu.make_async_copy(source, panel.at[pl.ds(slot, many), pl.ds(first, size)], sems.at[i])
        for i, (source, slot, many, first, size) in enumerate(plan)
    ]


def forward_kernel(
    row_ref, col_ref, rel_ref, count_ref, place_ref,
    p0, p1, p2, p3, arrived,
    w0, w1, w2, w3, w4, w5, w6, w7, w8, w9, w10,
    tiles_ref, hidden_ref, cot_ref,
    out_ref, grad_ref, mine_ref, send_ref,
    cols, totals, stacked, panel, col_sems, panel_sems,
):
    core, x = place_ref[0], place_ref[1]
    col_copies = [
        pltpu.make_async_copy(part, cols.at[pl.ds(2 * j, 2)], col_sems.at[j])
        for j, part in enumerate((p0, p1, p2, p3))
    ]
    col_copies.append(pltpu.make_async_copy(arrived, cols.at[pl.ds(LOCAL, 8)], col_sems.at[4]))
    pieces = (w0, w1, w2, w3, w4, w5, w6, w7, w8, w9, w10)
    weights = panel_copies(core, place_ref[2], pieces, panel, panel_sems)
    for copy in col_copies:
        copy.start()
    for copy in weights:
        copy.start()
    totals[...] = jnp.zeros_like(totals)
    for copy in col_copies:
        copy.wait()
    count = count_ref[0]

    def one_tile(i):
        col = col_ref[i]
        slot = jnp.where(
            col < LOCAL, 2 * ((col // 2 + 4 - x) % 4) + col % 2, col
        )
        target = jnp.where(i < count, row_ref[i] * RELS + rel_ref[i], 2 * RELS)
        totals[target] += jnp.dot(tiles_ref[i], cols[slot], preferred_element_type=F32)

    def four_tiles(step, carry):
        for k in range(4):
            one_tile(step * 4 + k)
        return carry

    lax.fori_loop(0, TILES // 4, four_tiles, 0)
    for rel in range(RELS):
        for block in range(2):
            stacked[rel, block * BLOCK : (block + 1) * BLOCK, :] = totals[
                block * RELS + rel
            ].astype(BF16)
    near = pl.multiple_of(core * HALF, HALF)
    far = pl.multiple_of((1 - core) * HALF, HALF)
    for rel in range(RELS):
        mine_ref[rel] = stacked[rel, :, pl.ds(near, HALF)]
        send_ref[rel] = stacked[rel, :, pl.ds(far, HALF)]
    for copy in weights:
        copy.wait()
    for n in range(4):
        cut = slice(n * 256, (n + 1) * 256)
        v = jnp.zeros((ROWS, 256), F32)
        for j in range(4):
            v += jnp.dot(stacked[(x + j) % 4], panel[j, :, cut], preferred_element_type=F32)
        square = v * v
        t = jnp.tanh(GELU_A * (v + GELU_B * (square * v)))
        cdf = 0.5 * (1.0 + t)
        slope = cdf + (0.5 * v) * (1.0 - t * t) * (GELU_A * (1.0 + (3.0 * GELU_B) * square))
        out_ref[:, cut] = (hidden_ref[:, cut].astype(F32) + v * cdf).astype(BF16)
        grad_ref[:, cut] = (cot_ref[:, cut].astype(F32) * slope).astype(BF16)


def backward_kernel(
    row_ref, col_ref, rel_ref, count_ref, place_ref,
    w0, w1, w2, w3, w4, w5, w6, w7, w8, w9, w10,
    tiles_ref, grad_ref,
    own_ref, right_a, right_b, left_a, left_b, opp_a, opp_b,
    grads, nodes, panel, panel_sems,
):
    core, x = place_ref[0], place_ref[1]
    pieces = (w0, w1, w2, w3, w4, w5, w6, w7, w8, w9, w10)
    weights = panel_copies(core, place_ref[2], pieces, panel, panel_sems)
    for copy in weights:
        copy.start()
    nodes[...] = jnp.zeros_like(nodes)
    for j in range(4):
        for copy in (weights[:1], weights[1:], (), ())[j]:
            copy.wait()
        rel = (x + j) % 4
        for n in range(4):
            cut = slice(n * 256, (n + 1) * 256)
            part = lax.dot_general(
                grad_ref[...], panel[j, cut, :], (((1,), (1,)), ((), ())),
                preferred_element_type=F32,
            ).astype(BF16)
            grads[rel, :, cut] = part[:BLOCK]
            grads[RELS + rel, :, cut] = part[BLOCK:]
    count = count_ref[0]

    def one_tile(i):
        col = col_ref[i]
        target = jnp.where((i < count) & (col < LOCAL), col, LOCAL)
        nodes[target] += lax.dot_general(
            tiles_ref[i], grads[row_ref[i] * RELS + rel_ref[i]], (((0,), (0,)), ((), ())),
            preferred_element_type=F32,
        )

    def four_tiles(step, carry):
        for k in range(4):
            one_tile(step * 4 + k)
        return carry

    lax.fori_loop(0, TILES // 4, four_tiles, 0)
    own_ref[:BLOCK] = nodes[2 * x]
    own_ref[BLOCK:] = nodes[2 * x + 1]
    for j, half_a, half_b in ((1, right_a, right_b), (3, left_a, left_b), (2, opp_a, opp_b)):
        owner = (x + j) % 4
        half_a[...] = nodes[2 * owner].astype(BF16)
        half_b[...] = nodes[2 * owner + 1].astype(BF16)


def panel_grad_kernel(parts, place_ref, mine_ref, came_ref, grad_ref, grad_came_ref, *outs):
    for (axis, j, first, size), out in zip(parts, outs):
        rel = (place_ref[axis] + j) % 4
        cut = slice(first, first + size)
        part = lax.dot_general(
            mine_ref[rel, :, cut], grad_ref[...], (((0,), (0,)), ((), ())),
            preferred_element_type=F32,
        ) + lax.dot_general(
            came_ref[rel, :, cut], grad_came_ref[...], (((0,), (0,)), ((), ())),
            preferred_element_type=F32,
        )
        out[...] = part.astype(out.dtype)


def struct(shape, dtype=BF16):
    return jax.ShapeDtypeStruct(shape, dtype)


def cost(flops, moved):
    return pl.CostEstimate(flops=flops, bytes_accessed=moved, transcendentals=0)


def params(mib=60):
    return pltpu.CompilerParams(vmem_limit_bytes=mib * 2**20)


def panel_grad(parts, dtypes, operands):
    return pl.pallas_call(
        functools.partial(panel_grad_kernel, parts),
        out_shape=[struct((p[3], WIDTH), d) for p, d in zip(parts, dtypes)],
        in_specs=[SMEM] + [VMEM] * 4,
        out_specs=[VMEM] * len(parts),
        compiler_params=params(),
        cost_estimate=cost(2 * 512 * WIDTH * sum(p[3] for p in parts), 6 << 20),
    )(*operands)


def add(a, b):
    return (a.astype(F32) + b.astype(F32)).astype(BF16)


def ring_first(axis, right, left, opposite):
    via_left = lax.ppermute(opposite[0], axis, NEXT)
    via_right = lax.ppermute(opposite[1], axis, BACK)
    right = jnp.concatenate([add(right[0], via_left), right[1]], 0)
    left = jnp.concatenate([left[0], add(left[1], via_right)], 0)
    return right, left


def ring_last(axis, own, right, left):
    got_left = lax.ppermute(right, axis, NEXT)
    got_right = lax.ppermute(left, axis, BACK)
    return own.astype(F32) + got_left.astype(F32) + got_right.astype(F32)


def on_device(
    hidden, history, cotangent, weight, send_index, send_count,
    tile_values, tile_row, tile_col, tile_rel, tile_count,
):
    core, x, y, z = (lax.axis_index(a) for a in ("c", "x", "y", "z"))
    place = jnp.stack([core, x, y, z]).astype(jnp.int32)
    slots = send_index.shape[2]
    peers = send_index.shape[1]

    usable = jnp.arange(slots, dtype=jnp.int32)[None, :] < send_count[0][:, None]
    wanted = jnp.where(usable, send_index[0], -1).reshape(-1)
    picks = (wanted[:, None] == jnp.arange(ROWS, dtype=jnp.int32)[None, :]).astype(BF16)
    fetched = jnp.dot(picks, history, preferred_element_type=F32).astype(BF16)
    swap = lambda a: lax.ppermute(a, "c", [(0, 1), (1, 0)])
    strip = HALF // 4
    own_strip = lax.dynamic_slice_in_dim(weight, core * HALF + y * strip, strip, 0)
    left = lax.ppermute(own_strip, "x", NEXT)
    right = lax.ppermute(own_strip, "x", BACK)
    fetched = fetched.reshape(peers, slots, WIDTH)
    fetched, left, right = lax.optimization_barrier((fetched, left, right))
    arrived = lax.all_to_all(fetched, ALL, split_axis=0, concat_axis=0, tiled=True)
    arrived = arrived.reshape(LOCAL, BLOCK, WIDTH)
    op_a = lax.ppermute(left[: strip // 2], "x", NEXT)
    op_b = lax.ppermute(right[strip // 2 :], "x", BACK)
    strips = jnp.concatenate([right, op_a, op_b, left], 0).reshape(3, strip, WIDTH)
    below = lax.ppermute(strips, "y", NEXT)
    above = lax.ppermute(strips, "y", BACK)
    p0 = hidden.reshape(2, BLOCK, WIDTH)
    p3 = lax.ppermute(p0, "x", NEXT)
    p1 = lax.ppermute(p0, "x", BACK)
    p1, p3, below, above = lax.optimization_barrier((p1, p3, below, above))
    p2 = jnp.concatenate(
        [lax.ppermute(p3[:1], "x", NEXT), lax.ppermute(p1[1:], "x", BACK)], 0
    )
    far_a = lax.ppermute(below[:, : strip // 2], "y", NEXT)
    far_b = lax.ppermute(above[:, strip // 2 :], "y", BACK)
    side = (strips, below, above, far_a, far_b)
    panel = (weight.reshape(1, WIDTH, WIDTH), *side, *(swap(a) for a in side))

    ids = (tile_row[0], tile_col[0], tile_rel[0], tile_count, place)
    values = tile_values[0]
    output, grad_preact, mine, to_send = pl.pallas_call(
        forward_kernel,
        out_shape=[
            struct((ROWS, WIDTH)),
            struct((ROWS, WIDTH)),
            struct((RELS, ROWS, HALF)),
            struct((RELS, ROWS, HALF)),
        ],
        in_specs=[SMEM] * 5 + [HBM] * 16 + [VMEM] * 3,
        out_specs=[VMEM] * 4,
        scratch_shapes=[
            pltpu.VMEM((16, BLOCK, WIDTH), BF16),
            pltpu.VMEM((2 * RELS + 1, BLOCK, WIDTH), F32),
            pltpu.VMEM((RELS, ROWS, WIDTH), BF16),
            pltpu.VMEM((RELS, WIDTH, WIDTH), BF16),
            pltpu.SemaphoreType.DMA((5,)),
            pltpu.SemaphoreType.DMA((11,)),
        ],
        compiler_params=params(),
        cost_estimate=cost(3 * 10**9, 20 << 20),
    )(*ids, p0, p1, p2, p3, arrived, *panel, values, hidden, cotangent)

    came = swap(to_send)
    grad_came = swap(grad_preact)

    operands = (place, mine, came, grad_preact, grad_came)
    outs = panel_grad(
        tuple((axis, j, first, 128) for axis, j, base in ((2, 2, 0), (1, 2, 256)) for first in (base, base + 128)),
        (BF16,) * 4,
        operands,
    )
    y_opp, x_opp = outs[:2], outs[2:]
    *outs, y_own, x_own = panel_grad(
        tuple(
            (axis, j, first, 128)
            for axis, base in ((2, 0), (1, 256))
            for j in (1, 3)
            for first in (base, base + 128)
        )
        + ((2, 0, 0, 256), (1, 0, 256, 256)),
        (BF16,) * 8 + (F32,) * 2,
        operands,
    )
    y_right, y_left = ring_first("y", outs[0:2], outs[2:4], y_opp)
    x_right, x_left = ring_first("x", outs[4:6], outs[6:8], x_opp)
    late_grad, y_right, y_left, x_right, x_left = lax.optimization_barrier(
        (grad_preact, y_right, y_left, x_right, x_left)
    )
    first = ring_last("y", y_own, y_right, y_left).reshape(4, 4, 16, WIDTH)
    second = ring_last("x", x_own, x_right, x_left).reshape(4, 4, 16, WIDTH)

    own, *node_parts = pl.pallas_call(
        backward_kernel,
        out_shape=[struct((ROWS, WIDTH), F32)]
        + [struct((BLOCK, WIDTH))] * 6,
        in_specs=[SMEM] * 5 + [HBM] * 11 + [VMEM] * 2,
        out_specs=[VMEM] * 7,
        scratch_shapes=[
            pltpu.VMEM((2 * RELS, BLOCK, WIDTH), BF16),
            pltpu.VMEM((LOCAL + 1, BLOCK, WIDTH), F32),
            pltpu.VMEM((RELS, WIDTH, WIDTH), BF16),
            pltpu.SemaphoreType.DMA((11,)),
        ],
        compiler_params=params(),
        cost_estimate=cost(3 * 10**9, 16 << 20),
    )(*ids, *panel, values, late_grad)
    def chunks(place_on, rows):
        chunk = lambda j: lax.dynamic_index_in_dim(rows, (place_on + j) % 4, 1, keepdims=False)
        halves = lambda j: (chunk(j)[:2].astype(BF16), chunk(j)[2:].astype(BF16))
        return chunk(0), halves(1), halves(3), halves(2)

    first_own, *first_parts = chunks(x, first)
    second_own, *second_parts = chunks(y, second)
    first_parts, second_parts, node_parts = lax.optimization_barrier(
        (first_parts, second_parts, node_parts)
    )
    first_sides = ring_first("x", *first_parts)
    second_sides = ring_first("y", *second_parts)
    node_sides = ring_first("x", node_parts[0:2], node_parts[2:4], node_parts[4:6])
    first_sides, second_sides, node_sides = lax.optimization_barrier(
        (first_sides, second_sides, node_sides)
    )
    pieces = jnp.concatenate(
        [ring_last("x", first_own, *first_sides), ring_last("y", second_own, *second_sides)], 0
    ).astype(BF16)
    grad_hidden = cotangent.astype(F32) + ring_last("x", own, *node_sides)

    def home(at_y, c, at_x, k):
        to_y, to_x = (at_y, at_x) if k < 4 else (at_x, at_y)
        return ((to_y * 8 + c * 4 + k // 2) * 2 + k % 2) * 4 + to_x

    def routes(pick):
        return [
            (((at_y * 8 + at_z) * 2 + c) * 4 + at_x, home(at_y, c, at_x, pick(at_z)))
            for at_y in range(4) for at_z in range(8) for c in range(2) for at_x in range(4)
        ]

    if Z_STEPS == 1:
        grad_weight = jnp.zeros((16, WIDTH), F32)
        for j in range(8):
            piece = lax.dynamic_index_in_dim(pieces, z ^ j, 0, keepdims=False)
            grad_weight += lax.ppermute(piece, ALL, routes(lambda at_z: at_z ^ j)).astype(F32)
        return (output, grad_hidden, grad_weight)
    grouped = pieces.reshape(2, 4, 16, WIDTH)
    low = z % 4
    pair = lax.dynamic_index_in_dim(grouped, low, 1, keepdims=False).astype(F32)
    for j in range(1, 4):
        sent = lax.dynamic_index_in_dim(grouped, low ^ j, 1, keepdims=False)
        pair += lax.ppermute(sent, "z", [(i, i ^ j) for i in range(8)]).astype(F32)
    pair = pair.astype(BF16)
    grad_weight = jnp.zeros((16, WIDTH), F32)
    for j in range(2):
        piece = lax.dynamic_index_in_dim(pair, (z // 4) ^ j, 0, keepdims=False)
        route = routes(lambda at_z: ((at_z // 4) ^ j) * 4 + at_z % 4)
        grad_weight += lax.ppermute(piece, ALL, route).astype(F32)
    return (output, grad_hidden, grad_weight)


def solution(mesh):
    physical = Mesh(mesh.devices.reshape(4, 8, 2, 4), ALL)
    rows = P(ALL, None)
    return jax.shard_map(
        on_device,
        mesh=physical,
        in_specs=(
            rows, rows, rows, P("x", None), P(ALL, None, None), rows,
            P(ALL, None, None, None), rows, rows, rows, P(ALL),
        ),
        out_specs=(rows, rows, rows),
        check_vma=False,
    )
```

```python
import functools

import jax
import jax.numpy as jnp
from jax import lax
from jax.experimental import pallas as pl
from jax.experimental.pallas import tpu as pltpu
from jax.sharding import Mesh, PartitionSpec as P

ROWS = 256
WIDTH = 1024
HALF = 512
RELS = 4
BLOCK = 128
TILES = 24
LOCAL = 8
ALL = ("y", "z", "c", "x")
F32 = jnp.float32
BF16 = jnp.bfloat16
NEXT = [(i, (i + 1) % 4) for i in range(4)]
BACK = [(i, (i + 3) % 4) for i in range(4)]
VMEM = pl.BlockSpec(memory_space=pltpu.VMEM)
HBM = pl.BlockSpec(memory_space=pltpu.HBM)
SMEM = pl.BlockSpec(memory_space=pltpu.SMEM)
GELU_A = 0.7978845608028654
GELU_B = 0.044715
Z_STEPS = 2
VM_F, VM_B, VM_C, VM_J = 60, 60, 16, 12


def panel_copies(core, y, pieces, panel, sems):
    near = core * HALF
    far = (1 - core) * HALF
    strip = HALF // 4
    plan = [(pieces[0], 0, 1, 0, WIDTH)]
    for base, side in ((near, pieces[1:6]), (far, pieces[6:11])):
        for piece, step, start, size in (
            (side[0], 0, 0, strip),
            (side[1], 3, 0, strip),
            (side[2], 1, 0, strip),
            (side[3], 2, 0, strip // 2),
            (side[4], 2, strip // 2, strip // 2),
        ):
            first = base + ((y + step) % 4) * strip + start
            plan.append((piece, 1, 3, pl.multiple_of(first, strip // 2), size))
    return [
        pltpu.make_async_copy(source, panel.at[pl.ds(slot, many), pl.ds(first, size)], sems.at[i])
        for i, (source, slot, many, first, size) in enumerate(plan)
    ]


def forward_kernel(
    row_ref, col_ref, rel_ref, count_ref, place_ref,
    p0, p1, p2, p3, arrived,
    w0, w1, w2, w3, w4, w5, w6, w7, w8, w9, w10,
    tiles_in, hidden_in, cot_in,
    out_ref, grad_ref, mine_ref, send_ref,
    tiles_ref, hidden_ref, cot_ref, cols, totals, stacked, panel, col_sems, panel_sems, row_sems,
):
    core, x = place_ref[0], place_ref[1]
    col_copies = [
        pltpu.make_async_copy(part, cols.at[pl.ds(first, part.shape[0])], col_sems.at[i])
        for i, (part, first) in enumerate(
            ((p0, 0), (p1, 2), (p2, 4), (p3, 6), (arrived, LOCAL))
        )
    ]
    pieces = (w0, w1, w2, w3, w4, w5, w6, w7, w8, w9, w10)
    weights = panel_copies(core, place_ref[2], pieces, panel, panel_sems)
    col_copies.append(pltpu.make_async_copy(tiles_in, tiles_ref, col_sems.at[5]))
    row_copies = [
        pltpu.make_async_copy(hidden_in, hidden_ref, row_sems.at[0]),
        pltpu.make_async_copy(cot_in, cot_ref, row_sems.at[1]),
    ]
    for copy in col_copies:
        copy.start()
    totals[...] = jnp.zeros_like(totals)
    for copy in col_copies:
        copy.wait()
    for copy in weights:
        copy.start()
    for copy in row_copies:
        copy.start()
    count = count_ref[0]

    def one_tile(i):
        col = col_ref[i]
        slot = jnp.where(
            col < LOCAL, 2 * ((col // 2 + 4 - x) % 4) + col % 2, col
        )
        target = jnp.where(i < count, row_ref[i] * RELS + rel_ref[i], 2 * RELS)
        totals[target] += jnp.dot(tiles_ref[i], cols[slot], preferred_element_type=F32)

    def four_tiles(step, carry):
        for k in range(4):
            one_tile(step * 4 + k)
        return carry

    lax.fori_loop(0, TILES // 4, four_tiles, 0)
    for rel in range(RELS):
        for block in range(2):
            stacked[rel, block * BLOCK : (block + 1) * BLOCK, :] = totals[
                block * RELS + rel
            ].astype(BF16)
    near = pl.multiple_of(core * HALF, HALF)
    far = pl.multiple_of((1 - core) * HALF, HALF)
    for rel in range(RELS):
        mine_ref[rel] = stacked[rel, :, pl.ds(near, HALF)]
        send_ref[rel] = stacked[rel, :, pl.ds(far, HALF)]
    for copy in weights:
        copy.wait()
    for copy in row_copies:
        copy.wait()
    for n in range(4):
        cut = slice(n * 256, (n + 1) * 256)
        v = jnp.zeros((ROWS, 256), F32)
        for j in range(4):
            v += jnp.dot(stacked[(x + j) % 4], panel[j, :, cut], preferred_element_type=F32)
        square = v * v
        t = jnp.tanh(GELU_A * (v + GELU_B * (square * v)))
        cdf = 0.5 * (1.0 + t)
        slope = cdf + (0.5 * v) * (1.0 - t * t) * (GELU_A * (1.0 + (3.0 * GELU_B) * square))
        out_ref[:, cut] = (hidden_ref[:, cut].astype(F32) + v * cdf).astype(BF16)
        grad_ref[:, cut] = (cot_ref[:, cut].astype(F32) * slope).astype(BF16)


def backward_kernel(
    row_ref, col_ref, rel_ref, count_ref, place_ref,
    w0, w1, w2, w3, w4, w5, w6, w7, w8, w9, w10,
    tiles_in, grad_in,
    own_ref, right_a, right_b, left_a, left_b, opp_a, opp_b,
    tiles_ref, grad_ref, grads, nodes, panel, panel_sems, row_sems,
):
    core, x = place_ref[0], place_ref[1]
    pieces = (w0, w1, w2, w3, w4, w5, w6, w7, w8, w9, w10)
    weights = panel_copies(core, place_ref[2], pieces, panel, panel_sems)
    rows_copy = pltpu.make_async_copy(grad_in, grad_ref, row_sems.at[0])
    tiles_copy = pltpu.make_async_copy(tiles_in, tiles_ref, row_sems.at[1])
    rows_copy.start()
    for copy in weights:
        copy.start()
    tiles_copy.start()
    rows_copy.wait()
    nodes[...] = jnp.zeros_like(nodes)
    for j in range(4):
        for copy in (weights[:1], weights[1:], (), ())[j]:
            copy.wait()
        rel = (x + j) % 4
        for n in range(4):
            cut = slice(n * 256, (n + 1) * 256)
            part = lax.dot_general(
                grad_ref[...], panel[j, cut, :], (((1,), (1,)), ((), ())),
                preferred_element_type=F32,
            ).astype(BF16)
            grads[rel, :, cut] = part[:BLOCK]
            grads[RELS + rel, :, cut] = part[BLOCK:]
    tiles_copy.wait()
    count = count_ref[0]

    def one_tile(i):
        col = col_ref[i]
        target = jnp.where((i < count) & (col < LOCAL), col, LOCAL)
        nodes[target] += lax.dot_general(
            tiles_ref[i], grads[row_ref[i] * RELS + rel_ref[i]], (((0,), (0,)), ((), ())),
            preferred_element_type=F32,
        )

    def four_tiles(step, carry):
        for k in range(4):
            one_tile(step * 4 + k)
        return carry

    lax.fori_loop(0, TILES // 4, four_tiles, 0)
    own_ref[:BLOCK] = nodes[2 * x]
    own_ref[BLOCK:] = nodes[2 * x + 1]
    for j, half_a, half_b in ((1, right_a, right_b), (3, left_a, left_b), (2, opp_a, opp_b)):
        owner = (x + j) % 4
        half_a[...] = nodes[2 * owner].astype(BF16)
        half_b[...] = nodes[2 * owner + 1].astype(BF16)


def panel_grad_kernel(parts, place_ref, mine_ref, came_ref, grad_ref, grad_came_ref, *outs):
    for (axis, j, first, size), out in zip(parts, outs):
        rel = (place_ref[axis] + j) % 4
        cut = slice(first, first + size)
        part = lax.dot_general(
            mine_ref[rel, :, cut], grad_ref[...], (((0,), (0,)), ((), ())),
            preferred_element_type=F32,
        ) + lax.dot_general(
            came_ref[rel, :, cut], grad_came_ref[...], (((0,), (0,)), ((), ())),
            preferred_element_type=F32,
        )
        out[...] = part.astype(out.dtype)


def struct(shape, dtype=BF16):
    return jax.ShapeDtypeStruct(shape, dtype)


def cost(flops, moved):
    return pl.CostEstimate(flops=flops, bytes_accessed=moved, transcendentals=0)


def params(mib=60):
    return pltpu.CompilerParams(vmem_limit_bytes=mib * 2**20)


def panel_grad(parts, dtypes, operands):
    return pl.pallas_call(
        functools.partial(panel_grad_kernel, parts),
        out_shape=[struct((p[3], WIDTH), d) for p, d in zip(parts, dtypes)],
        in_specs=[SMEM] + [VMEM] * 4,
        out_specs=[VMEM] * len(parts),
        compiler_params=params(VM_C),
        cost_estimate=cost(2 * 512 * WIDTH * sum(p[3] for p in parts), 6 << 20),
    )(*operands)


def join_kernel(count, *refs):
    for i in range(count):
        top, low, via, out = refs[3 * i], refs[3 * i + 1], refs[3 * i + 2], refs[3 * count + i]
        half = top.shape[0]
        summed = ((low if i % 2 else top)[...].astype(F32) + via[...].astype(F32)).astype(BF16)
        out[:half] = top[...] if i % 2 else summed
        out[half:] = summed if i % 2 else low[...]


def join(*chunks):
    count = len(chunks)
    half = chunks[0][0].shape[0]
    return pl.pallas_call(
        functools.partial(join_kernel, count),
        out_shape=[struct((2 * half, WIDTH))] * count,
        in_specs=[VMEM] * (3 * count),
        out_specs=[VMEM] * count,
        compiler_params=params(VM_J),
        cost_estimate=cost(10**6, 5 << 20),
    )(*(a for chunk in chunks for a in chunk))


def through(axis, opposite):
    return lax.ppermute(opposite[0], axis, NEXT), lax.ppermute(opposite[1], axis, BACK)


def ring_last(axis, own, right, left):
    got_left = lax.ppermute(right, axis, NEXT)
    got_right = lax.ppermute(left, axis, BACK)
    return own.astype(F32) + got_left.astype(F32) + got_right.astype(F32)


def forward_call(ids, parts, arrived, panel, values, hidden, cotangent):
    return pl.pallas_call(
        forward_kernel,
        out_shape=[
            struct((ROWS, WIDTH)),
            struct((ROWS, WIDTH)),
            struct((RELS, ROWS, HALF)),
            struct((RELS, ROWS, HALF)),
        ],
        in_specs=[SMEM] * 5 + [HBM] * 19,
        out_specs=[VMEM] * 4,
        scratch_shapes=[
            pltpu.VMEM((TILES, BLOCK, BLOCK), BF16),
            pltpu.VMEM((ROWS, WIDTH), BF16),
            pltpu.VMEM((ROWS, WIDTH), BF16),
            pltpu.VMEM((16, BLOCK, WIDTH), BF16),
            pltpu.VMEM((2 * RELS + 1, BLOCK, WIDTH), F32),
            pltpu.VMEM((RELS, ROWS, WIDTH), BF16),
            pltpu.VMEM((RELS, WIDTH, WIDTH), BF16),
            pltpu.SemaphoreType.DMA((6,)),
            pltpu.SemaphoreType.DMA((11,)),
            pltpu.SemaphoreType.DMA((2,)),
        ],
        compiler_params=params(VM_F),
        cost_estimate=cost(3 * 10**9, 20 << 20),
    )(*ids, *parts, arrived, *panel, values, hidden, cotangent)


def backward_call(ids, panel, values, grad_preact):
    return pl.pallas_call(
        backward_kernel,
        out_shape=[struct((ROWS, WIDTH), F32)] + [struct((BLOCK, WIDTH))] * 6,
        in_specs=[SMEM] * 5 + [HBM] * 13,
        out_specs=[VMEM] * 7,
        scratch_shapes=[
            pltpu.VMEM((TILES, BLOCK, BLOCK), BF16),
            pltpu.VMEM((ROWS, WIDTH), BF16),
            pltpu.VMEM((2 * RELS, BLOCK, WIDTH), BF16),
            pltpu.VMEM((LOCAL + 1, BLOCK, WIDTH), F32),
            pltpu.VMEM((RELS, WIDTH, WIDTH), BF16),
            pltpu.SemaphoreType.DMA((11,)),
            pltpu.SemaphoreType.DMA((2,)),
        ],
        compiler_params=params(VM_B),
        cost_estimate=cost(3 * 10**9, 16 << 20),
    )(*ids, *panel, values, grad_preact)


def on_device(
    hidden, history, cotangent, weight, send_index, send_count,
    tile_values, tile_row, tile_col, tile_rel, tile_count,
):
    core, x, y, z = (lax.axis_index(a) for a in ("c", "x", "y", "z"))
    place = jnp.stack([core, x, y, z]).astype(jnp.int32)
    slots = send_index.shape[2]
    peers = send_index.shape[1]

    usable = jnp.arange(slots, dtype=jnp.int32)[None, :] < send_count[0][:, None]
    wanted = jnp.where(usable, send_index[0], -1).reshape(-1)
    picks = (wanted[:, None] == jnp.arange(ROWS, dtype=jnp.int32)[None, :]).astype(BF16)
    fetched = jnp.dot(picks, history, preferred_element_type=F32).astype(BF16)
    swap = lambda a: lax.ppermute(a, "c", [(0, 1), (1, 0)])
    strip = HALF // 4
    own_strip = lax.dynamic_slice_in_dim(weight, core * HALF + y * strip, strip, 0)
    left = lax.ppermute(own_strip, "x", NEXT)
    right = lax.ppermute(own_strip, "x", BACK)
    fetched = fetched.reshape(peers, slots, WIDTH)
    fetched, left, right = lax.optimization_barrier((fetched, left, right))
    arrived = lax.all_to_all(fetched, ALL, split_axis=0, concat_axis=0, tiled=True)
    arrived = arrived.reshape(LOCAL, BLOCK, WIDTH)
    op_a = lax.ppermute(left[: strip // 2], "x", NEXT)
    op_b = lax.ppermute(right[strip // 2 :], "x", BACK)
    strips = jnp.concatenate([right, op_a, op_b, left], 0).reshape(3, strip, WIDTH)
    below = lax.ppermute(strips, "y", NEXT)
    above = lax.ppermute(strips, "y", BACK)
    p0 = hidden.reshape(2, BLOCK, WIDTH)
    p3, p2, p1 = (
        lax.ppermute(p0, "x", [(i, (i + step) % 4) for i in range(4)]) for step in (1, 2, 3)
    )
    far_a, far_b = below[:, : strip // 2], above[:, strip // 2 :]
    far_a, far_b = lax.optimization_barrier((far_a, far_b))
    far_a = lax.ppermute(far_a, "y", NEXT)
    far_b = lax.ppermute(far_b, "y", BACK)
    side = (strips, below, above, far_a, far_b)
    panel = (weight.reshape(1, WIDTH, WIDTH), *side, *(swap(a) for a in side))

    ids = (tile_row[0], tile_col[0], tile_rel[0], tile_count, place)
    values = tile_values[0]
    parts = (p0, p1, p2, p3)
    output, grad_preact, mine, to_send = forward_call(
        ids, parts, arrived, panel, values, hidden, cotangent
    )

    came = swap(to_send)
    grad_came = swap(grad_preact)

    operands = (place, mine, came, grad_preact, grad_came)
    outs = panel_grad(
        tuple((axis, j, first, 128) for axis, j, base in ((2, 2, 0), (1, 2, 256)) for first in (base, base + 128)),
        (BF16,) * 4,
        operands,
    )
    y_opp, x_opp = outs[:2], outs[2:]
    *outs, y_own, x_own = panel_grad(
        tuple(
            (axis, j, first, 128)
            for axis, base in ((2, 0), (1, 256))
            for j in (1, 3)
            for first in (base, base + 128)
        )
        + ((2, 0, 0, 256), (1, 0, 256, 256)),
        (BF16,) * 8 + (F32,) * 2,
        operands,
    )
    y_via, x_via = through("y", y_opp), through("x", x_opp)
    y_right, y_left, x_right, x_left = join(
        (*outs[0:2], y_via[0]), (*outs[2:4], y_via[1]), (*outs[4:6], x_via[0]), (*outs[6:8], x_via[1])
    )
    late_grad, y_right, y_left, x_right, x_left = lax.optimization_barrier(
        (grad_preact, y_right, y_left, x_right, x_left)
    )
    first = ring_last("y", y_own, y_right, y_left).reshape(4, 4, 16, WIDTH)
    second = ring_last("x", x_own, x_right, x_left).reshape(4, 4, 16, WIDTH)

    own, *node_parts = backward_call(ids, panel, values, late_grad)

    def chunks(place_on, rows):
        chunk = lambda j: lax.dynamic_index_in_dim(rows, (place_on + j) % 4, 1, keepdims=False)
        return chunk(0), tuple(chunk(j).astype(BF16) for j in (1, 2, 3))

    def arrivals(axis, own, sent):
        for j, chunk in zip((1, 2, 3), sent):
            own = own + lax.ppermute(chunk, axis, [(i, (i + j) % 4) for i in range(4)]).astype(F32)
        return own

    first_own, first_sent = chunks(x, first)
    second_own, second_sent = chunks(y, second)
    first_sent, second_sent, node_parts = lax.optimization_barrier(
        (first_sent, second_sent, node_parts)
    )
    pieces = jnp.concatenate(
        [arrivals("x", first_own, first_sent), arrivals("y", second_own, second_sent)], 0
    ).astype(BF16)
    pieces, node_parts = lax.optimization_barrier((pieces, node_parts))
    node_via = through("x", node_parts[4:6])
    node_sides = join((*node_parts[0:2], node_via[0]), (*node_parts[2:4], node_via[1]))
    grad_hidden = cotangent.astype(F32) + ring_last("x", own, *node_sides)

    def home(at_y, c, at_x, k):
        to_y, to_x = (at_y, at_x) if k < 4 else (at_x, at_y)
        return ((to_y * 8 + c * 4 + k // 2) * 2 + k % 2) * 4 + to_x

    def routes(pick):
        return [
            (((at_y * 8 + at_z) * 2 + c) * 4 + at_x, home(at_y, c, at_x, pick(at_z)))
            for at_y in range(4) for at_z in range(8) for c in range(2) for at_x in range(4)
        ]

    if Z_STEPS == 1:
        grad_weight = jnp.zeros((16, WIDTH), F32)
        for j in range(8):
            piece = lax.dynamic_index_in_dim(pieces, z ^ j, 0, keepdims=False)
            grad_weight += lax.ppermute(piece, ALL, routes(lambda at_z: at_z ^ j)).astype(F32)
        return (output, grad_hidden, grad_weight)
    grouped = pieces.reshape(2, 4, 16, WIDTH)
    low = z % 4
    pair = lax.dynamic_index_in_dim(grouped, low, 1, keepdims=False).astype(F32)
    for j in range(1, 4):
        sent = lax.dynamic_index_in_dim(grouped, low ^ j, 1, keepdims=False)
        pair += lax.ppermute(sent, "z", [(i, i ^ j) for i in range(8)]).astype(F32)
    pair = pair.astype(BF16)
    grad_weight = jnp.zeros((16, WIDTH), F32)
    for j in range(2):
        piece = lax.dynamic_index_in_dim(pair, (z // 4) ^ j, 0, keepdims=False)
        route = routes(lambda at_z: ((at_z // 4) ^ j) * 4 + at_z % 4)
        grad_weight += lax.ppermute(piece, ALL, route).astype(F32)
    return (output, grad_hidden, grad_weight)


def solution(mesh):
    physical = Mesh(mesh.devices.reshape(4, 8, 2, 4), ALL)
    rows = P(ALL, None)
    return jax.shard_map(
        on_device,
        mesh=physical,
        in_specs=(
            rows, rows, rows, P("x", None), P(ALL, None, None), rows,
            P(ALL, None, None, None), rows, rows, rows, P(ALL),
        ),
        out_specs=(rows, rows, rows),
        check_vma=False,
    )
```

```python
import functools

import jax
import jax.numpy as jnp
from jax import lax
from jax.experimental import pallas as pl
from jax.experimental.pallas import tpu as pltpu
from jax.sharding import Mesh, PartitionSpec as P

ROWS = 256
WIDTH = 1024
HALF = 512
RELS = 4
BLOCK = 128
TILES = 24
LOCAL = 8
ALL = ("y", "z", "c", "x")
F32 = jnp.float32
BF16 = jnp.bfloat16
NEXT = [(i, (i + 1) % 4) for i in range(4)]
BACK = [(i, (i + 3) % 4) for i in range(4)]
VMEM = pl.BlockSpec(memory_space=pltpu.VMEM)
HBM = pl.BlockSpec(memory_space=pltpu.HBM)
SMEM = pl.BlockSpec(memory_space=pltpu.SMEM)
GELU_A = 0.7978845608028654
GELU_B = 0.044715
Z_STEPS = 2
VM_F, VM_B, VM_C, VM_J = 60, 60, 16, 12


def panel_copies(core, y, pieces, panel, sems):
    near = core * HALF
    far = (1 - core) * HALF
    strip = HALF // 4
    half = strip // 2
    plan = [(pieces[0], 0, 1, 0, WIDTH)]
    for base, side in ((near, pieces[1:8]), (far, pieces[8:15])):
        for piece, step, start, size in zip(
            side, (0, 3, 3, 1, 1, 2, 2), (0, 0, half, 0, half, 0, half), (strip,) + (half,) * 6
        ):
            first = base + ((y + step) % 4) * strip + start
            plan.append((piece, 1, 3, pl.multiple_of(first, half), size))
    return [
        pltpu.make_async_copy(source, panel.at[pl.ds(slot, many), pl.ds(first, size)], sems.at[i])
        for i, (source, slot, many, first, size) in enumerate(plan)
    ]


def forward_kernel(
    row_ref, col_ref, rel_ref, count_ref, place_ref,
    p0, p1, p2, p3, arrived,
    w0, w1, w2, w3, w4, w5, w6, w7, w8, w9, w10, w11, w12, w13, w14,
    tiles_in, hidden_in, cot_in,
    out_ref, grad_ref, mine_ref, send_ref,
    tiles_ref, hidden_ref, cot_ref, cols, totals, stacked, panel, col_sems, panel_sems, row_sems,
):
    core, x = place_ref[0], place_ref[1]
    col_copies = [
        pltpu.make_async_copy(part, cols.at[pl.ds(first, part.shape[0])], col_sems.at[i])
        for i, (part, first) in enumerate(
            ((p0, 0), (p1, 2), (p2, 4), (p3, 6), (arrived, LOCAL))
        )
    ]
    pieces = (w0, w1, w2, w3, w4, w5, w6, w7, w8, w9, w10, w11, w12, w13, w14)
    weights = panel_copies(core, place_ref[2], pieces, panel, panel_sems)
    col_copies.append(pltpu.make_async_copy(tiles_in, tiles_ref, col_sems.at[5]))
    row_copies = [
        pltpu.make_async_copy(hidden_in, hidden_ref, row_sems.at[0]),
        pltpu.make_async_copy(cot_in, cot_ref, row_sems.at[1]),
    ]
    for copy in col_copies:
        copy.start()
    totals[...] = jnp.zeros_like(totals)
    for copy in col_copies:
        copy.wait()
    for copy in weights:
        copy.start()
    for copy in row_copies:
        copy.start()
    count = count_ref[0]

    def one_tile(i):
        col = col_ref[i]
        slot = jnp.where(
            col < LOCAL, 2 * ((col // 2 + 4 - x) % 4) + col % 2, col
        )
        target = jnp.where(i < count, row_ref[i] * RELS + rel_ref[i], 2 * RELS)
        totals[target] += jnp.dot(tiles_ref[i], cols[slot], preferred_element_type=F32)

    def four_tiles(step, carry):
        for k in range(4):
            one_tile(step * 4 + k)
        return carry

    lax.fori_loop(0, TILES // 4, four_tiles, 0)
    for rel in range(RELS):
        for block in range(2):
            stacked[rel, block * BLOCK : (block + 1) * BLOCK, :] = totals[
                block * RELS + rel
            ].astype(BF16)
    near = pl.multiple_of(core * HALF, HALF)
    far = pl.multiple_of((1 - core) * HALF, HALF)
    for rel in range(RELS):
        mine_ref[rel] = stacked[rel, :, pl.ds(near, HALF)]
        send_ref[rel] = stacked[rel, :, pl.ds(far, HALF)]
    for copy in weights:
        copy.wait()
    for copy in row_copies:
        copy.wait()
    for n in range(4):
        cut = slice(n * 256, (n + 1) * 256)
        v = jnp.zeros((ROWS, 256), F32)
        for j in range(4):
            v += jnp.dot(stacked[(x + j) % 4], panel[j, :, cut], preferred_element_type=F32)
        square = v * v
        t = jnp.tanh(GELU_A * (v + GELU_B * (square * v)))
        cdf = 0.5 * (1.0 + t)
        slope = cdf + (0.5 * v) * (1.0 - t * t) * (GELU_A * (1.0 + (3.0 * GELU_B) * square))
        out_ref[:, cut] = (hidden_ref[:, cut].astype(F32) + v * cdf).astype(BF16)
        grad_ref[:, cut] = (cot_ref[:, cut].astype(F32) * slope).astype(BF16)


def backward_kernel(
    row_ref, col_ref, rel_ref, count_ref, place_ref,
    w0, w1, w2, w3, w4, w5, w6, w7, w8, w9, w10, w11, w12, w13, w14,
    tiles_in, grad_in,
    own_ref, right_a, right_b, left_a, left_b, opp_a, opp_b,
    tiles_ref, grad_ref, grads, nodes, panel, panel_sems, row_sems,
):
    core, x = place_ref[0], place_ref[1]
    pieces = (w0, w1, w2, w3, w4, w5, w6, w7, w8, w9, w10, w11, w12, w13, w14)
    weights = panel_copies(core, place_ref[2], pieces, panel, panel_sems)
    rows_copy = pltpu.make_async_copy(grad_in, grad_ref, row_sems.at[0])
    tiles_copy = pltpu.make_async_copy(tiles_in, tiles_ref, row_sems.at[1])
    rows_copy.start()
    for copy in weights:
        copy.start()
    tiles_copy.start()
    rows_copy.wait()
    nodes[...] = jnp.zeros_like(nodes)
    for j in range(4):
        for copy in (weights[:1], weights[1:], (), ())[j]:
            copy.wait()
        rel = (x + j) % 4
        for n in range(4):
            cut = slice(n * 256, (n + 1) * 256)
            part = lax.dot_general(
                grad_ref[...], panel[j, cut, :], (((1,), (1,)), ((), ())),
                preferred_element_type=F32,
            ).astype(BF16)
            grads[rel, :, cut] = part[:BLOCK]
            grads[RELS + rel, :, cut] = part[BLOCK:]
    tiles_copy.wait()
    count = count_ref[0]

    def one_tile(i):
        col = col_ref[i]
        target = jnp.where((i < count) & (col < LOCAL), col, LOCAL)
        nodes[target] += lax.dot_general(
            tiles_ref[i], grads[row_ref[i] * RELS + rel_ref[i]], (((0,), (0,)), ((), ())),
            preferred_element_type=F32,
        )

    def four_tiles(step, carry):
        for k in range(4):
            one_tile(step * 4 + k)
        return carry

    lax.fori_loop(0, TILES // 4, four_tiles, 0)
    own_ref[:BLOCK] = nodes[2 * x]
    own_ref[BLOCK:] = nodes[2 * x + 1]
    for j, half_a, half_b in ((1, right_a, right_b), (3, left_a, left_b), (2, opp_a, opp_b)):
        owner = (x + j) % 4
        half_a[...] = nodes[2 * owner].astype(BF16)
        half_b[...] = nodes[2 * owner + 1].astype(BF16)


def panel_grad_kernel(parts, place_ref, mine_ref, came_ref, grad_ref, grad_came_ref, *outs):
    for (axis, j, first, size), out in zip(parts, outs):
        rel = (place_ref[axis] + j) % 4
        cut = slice(first, first + size)
        part = lax.dot_general(
            mine_ref[rel, :, cut], grad_ref[...], (((0,), (0,)), ((), ())),
            preferred_element_type=F32,
        ) + lax.dot_general(
            came_ref[rel, :, cut], grad_came_ref[...], (((0,), (0,)), ((), ())),
            preferred_element_type=F32,
        )
        out[...] = part.astype(out.dtype)


def struct(shape, dtype=BF16):
    return jax.ShapeDtypeStruct(shape, dtype)


def cost(flops, moved):
    return pl.CostEstimate(flops=flops, bytes_accessed=moved, transcendentals=0)


def params(mib=60):
    return pltpu.CompilerParams(vmem_limit_bytes=mib * 2**20)


def panel_grad(parts, dtypes, operands):
    return pl.pallas_call(
        functools.partial(panel_grad_kernel, parts),
        out_shape=[struct((p[3], WIDTH), d) for p, d in zip(parts, dtypes)],
        in_specs=[SMEM] + [VMEM] * 4,
        out_specs=[VMEM] * len(parts),
        compiler_params=params(VM_C),
        cost_estimate=cost(2 * 512 * WIDTH * sum(p[3] for p in parts), 6 << 20),
    )(*operands)


def join_kernel(count, *refs):
    for i in range(count):
        top, low, via, out = refs[3 * i], refs[3 * i + 1], refs[3 * i + 2], refs[3 * count + i]
        half = top.shape[0]
        summed = ((low if i % 2 else top)[...].astype(F32) + via[...].astype(F32)).astype(BF16)
        out[:half] = top[...] if i % 2 else summed
        out[half:] = summed if i % 2 else low[...]


def join(*chunks):
    count = len(chunks)
    half = chunks[0][0].shape[0]
    return pl.pallas_call(
        functools.partial(join_kernel, count),
        out_shape=[struct((2 * half, WIDTH))] * count,
        in_specs=[VMEM] * (3 * count),
        out_specs=[VMEM] * count,
        compiler_params=params(VM_J),
        cost_estimate=cost(10**6, 5 << 20),
    )(*(a for chunk in chunks for a in chunk))


def through(axis, opposite):
    return lax.ppermute(opposite[0], axis, NEXT), lax.ppermute(opposite[1], axis, BACK)


def ring_last(axis, own, right, left):
    got_left = lax.ppermute(right, axis, NEXT)
    got_right = lax.ppermute(left, axis, BACK)
    return own.astype(F32) + got_left.astype(F32) + got_right.astype(F32)


def forward_call(ids, parts, arrived, panel, values, hidden, cotangent):
    return pl.pallas_call(
        forward_kernel,
        out_shape=[
            struct((ROWS, WIDTH)),
            struct((ROWS, WIDTH)),
            struct((RELS, ROWS, HALF)),
            struct((RELS, ROWS, HALF)),
        ],
        in_specs=[SMEM] * 5 + [HBM] * 23,
        out_specs=[VMEM] * 4,
        scratch_shapes=[
            pltpu.VMEM((TILES, BLOCK, BLOCK), BF16),
            pltpu.VMEM((ROWS, WIDTH), BF16),
            pltpu.VMEM((ROWS, WIDTH), BF16),
            pltpu.VMEM((16, BLOCK, WIDTH), BF16),
            pltpu.VMEM((2 * RELS + 1, BLOCK, WIDTH), F32),
            pltpu.VMEM((RELS, ROWS, WIDTH), BF16),
            pltpu.VMEM((RELS, WIDTH, WIDTH), BF16),
            pltpu.SemaphoreType.DMA((6,)),
            pltpu.SemaphoreType.DMA((15,)),
            pltpu.SemaphoreType.DMA((2,)),
        ],
        compiler_params=params(VM_F),
        cost_estimate=cost(3 * 10**9, 20 << 20),
    )(*ids, *parts, arrived, *panel, values, hidden, cotangent)


def backward_call(ids, panel, values, grad_preact):
    return pl.pallas_call(
        backward_kernel,
        out_shape=[struct((ROWS, WIDTH), F32)] + [struct((BLOCK, WIDTH))] * 6,
        in_specs=[SMEM] * 5 + [HBM] * 17,
        out_specs=[VMEM] * 7,
        scratch_shapes=[
            pltpu.VMEM((TILES, BLOCK, BLOCK), BF16),
            pltpu.VMEM((ROWS, WIDTH), BF16),
            pltpu.VMEM((2 * RELS, BLOCK, WIDTH), BF16),
            pltpu.VMEM((LOCAL + 1, BLOCK, WIDTH), F32),
            pltpu.VMEM((RELS, WIDTH, WIDTH), BF16),
            pltpu.SemaphoreType.DMA((15,)),
            pltpu.SemaphoreType.DMA((2,)),
        ],
        compiler_params=params(VM_B),
        cost_estimate=cost(3 * 10**9, 16 << 20),
    )(*ids, *panel, values, grad_preact)


def on_device(
    hidden, history, cotangent, weight, send_index, send_count,
    tile_values, tile_row, tile_col, tile_rel, tile_count,
):
    core, x, y, z = (lax.axis_index(a) for a in ("c", "x", "y", "z"))
    place = jnp.stack([core, x, y, z]).astype(jnp.int32)
    slots = send_index.shape[2]
    peers = send_index.shape[1]

    usable = jnp.arange(slots, dtype=jnp.int32)[None, :] < send_count[0][:, None]
    wanted = jnp.where(usable, send_index[0], -1).reshape(-1)
    picks = (wanted[:, None] == jnp.arange(ROWS, dtype=jnp.int32)[None, :]).astype(BF16)
    fetched = jnp.dot(picks, history, preferred_element_type=F32).astype(BF16)
    swap = lambda a: lax.ppermute(a, "c", [(0, 1), (1, 0)])
    strip = HALF // 4
    own_strip = lax.dynamic_slice_in_dim(weight, core * HALF + y * strip, strip, 0)
    left = lax.ppermute(own_strip, "x", NEXT)
    right = lax.ppermute(own_strip, "x", BACK)
    fetched = fetched.reshape(peers, slots, WIDTH)
    fetched, left, right = lax.optimization_barrier((fetched, left, right))
    arrived = lax.all_to_all(fetched, ALL, split_axis=0, concat_axis=0, tiled=True)
    arrived = arrived.reshape(LOCAL, BLOCK, WIDTH)
    op_a = lax.ppermute(left[: strip // 2], "x", NEXT)
    op_b = lax.ppermute(right[strip // 2 :], "x", BACK)
    strips = jnp.concatenate([right, op_a, op_b, left], 0).reshape(3, strip, WIDTH)
    upper, lower = strips[:, : strip // 2], strips[:, strip // 2 :]
    below_a = lax.ppermute(upper, "y", NEXT)
    above_b = lax.ppermute(lower, "y", BACK)
    below_b = lax.ppermute(lower, "y", NEXT)
    above_a = lax.ppermute(upper, "y", BACK)
    p0 = hidden.reshape(2, BLOCK, WIDTH)
    p3, p2, p1 = (
        lax.ppermute(p0, "x", [(i, (i + step) % 4) for i in range(4)]) for step in (1, 2, 3)
    )
    far_a = lax.ppermute(below_a, "y", NEXT)
    far_b = lax.ppermute(above_b, "y", BACK)
    side = (strips, below_a, below_b, above_a, above_b, far_a, far_b)
    panel = (weight.reshape(1, WIDTH, WIDTH), *side, *(swap(a) for a in side))

    ids = (tile_row[0], tile_col[0], tile_rel[0], tile_count, place)
    values = tile_values[0]
    parts = (p0, p1, p2, p3)
    output, grad_preact, mine, to_send = forward_call(
        ids, parts, arrived, panel, values, hidden, cotangent
    )

    came = swap(to_send)
    grad_came = swap(grad_preact)

    operands = (place, mine, came, grad_preact, grad_came)
    outs = panel_grad(
        tuple((axis, j, first, 128) for axis, j, base in ((2, 2, 0), (1, 2, 256)) for first in (base, base + 128)),
        (BF16,) * 4,
        operands,
    )
    y_opp, x_opp = outs[:2], outs[2:]
    *outs, y_own, x_own = panel_grad(
        tuple(
            (axis, j, first, 128)
            for axis, base in ((2, 0), (1, 256))
            for j in (1, 3)
            for first in (base, base + 128)
        )
        + ((2, 0, 0, 256), (1, 0, 256, 256)),
        (BF16,) * 8 + (F32,) * 2,
        operands,
    )
    y_via, x_via = through("y", y_opp), through("x", x_opp)
    y_right, y_left, x_right, x_left = join(
        (*outs[0:2], y_via[0]), (*outs[2:4], y_via[1]), (*outs[4:6], x_via[0]), (*outs[6:8], x_via[1])
    )
    late_grad, y_right, y_left, x_right, x_left = lax.optimization_barrier(
        (grad_preact, y_right, y_left, x_right, x_left)
    )
    first = ring_last("y", y_own, y_right, y_left).reshape(4, 4, 16, WIDTH)
    second = ring_last("x", x_own, x_right, x_left).reshape(4, 4, 16, WIDTH)

    own, *node_parts = backward_call(ids, panel, values, late_grad)

    def chunks(place_on, rows):
        chunk = lambda j: lax.dynamic_index_in_dim(rows, (place_on + j) % 4, 1, keepdims=False)
        return chunk(0), tuple(chunk(j).astype(BF16) for j in (1, 2, 3))

    def arrivals(axis, own, sent):
        for j, chunk in zip((1, 2, 3), sent):
            own = own + lax.ppermute(chunk, axis, [(i, (i + j) % 4) for i in range(4)]).astype(F32)
        return own

    first_own, first_sent = chunks(x, first)
    second_own, second_sent = chunks(y, second)
    first_sent, second_sent, node_parts = lax.optimization_barrier(
        (first_sent, second_sent, node_parts)
    )
    pieces = jnp.concatenate(
        [arrivals("x", first_own, first_sent), arrivals("y", second_own, second_sent)], 0
    ).astype(BF16)
    pieces, node_parts = lax.optimization_barrier((pieces, node_parts))
    node_via = through("x", node_parts[4:6])
    node_sides = join((*node_parts[0:2], node_via[0]), (*node_parts[2:4], node_via[1]))
    grad_hidden = cotangent.astype(F32) + ring_last("x", own, *node_sides)

    def home(at_y, c, at_x, k):
        to_y, to_x = (at_y, at_x) if k < 4 else (at_x, at_y)
        return ((to_y * 8 + c * 4 + k // 2) * 2 + k % 2) * 4 + to_x

    def routes(pick):
        return [
            (((at_y * 8 + at_z) * 2 + c) * 4 + at_x, home(at_y, c, at_x, pick(at_z)))
            for at_y in range(4) for at_z in range(8) for c in range(2) for at_x in range(4)
        ]

    if Z_STEPS == 1:
        grad_weight = jnp.zeros((16, WIDTH), F32)
        for j in range(8):
            piece = lax.dynamic_index_in_dim(pieces, z ^ j, 0, keepdims=False)
            grad_weight += lax.ppermute(piece, ALL, routes(lambda at_z: at_z ^ j)).astype(F32)
        return (output, grad_hidden, grad_weight)
    grouped = pieces.reshape(2, 4, 16, WIDTH)
    low = z % 4
    pair = lax.dynamic_index_in_dim(grouped, low, 1, keepdims=False).astype(F32)
    for j in range(1, 4):
        sent = lax.dynamic_index_in_dim(grouped, low ^ j, 1, keepdims=False)
        pair += lax.ppermute(sent, "z", [(i, i ^ j) for i in range(8)]).astype(F32)
    pair = pair.astype(BF16)
    grad_weight = jnp.zeros((16, WIDTH), F32)
    for j in range(2):
        piece = lax.dynamic_index_in_dim(pair, (z // 4) ^ j, 0, keepdims=False)
        route = routes(lambda at_z: ((at_z // 4) ^ j) * 4 + at_z % 4)
        grad_weight += lax.ppermute(piece, ALL, route).astype(F32)
    return (output, grad_hidden, grad_weight)


def solution(mesh):
    physical = Mesh(mesh.devices.reshape(4, 8, 2, 4), ALL)
    rows = P(ALL, None)
    return jax.shard_map(
        on_device,
        mesh=physical,
        in_specs=(
            rows, rows, rows, P("x", None), P(ALL, None, None), rows,
            P(ALL, None, None, None), rows, rows, rows, P(ALL),
        ),
        out_specs=(rows, rows, rows),
        check_vma=False,
    )
```
